32 devices in a mesh: ctx: 8 (over z, x), grp: 4 (over y, core).
Axes of the slice: x: 2, y: 2, z: 4, core: 2. Of those that a mesh axis runs over, the one named last changes fastest.
Arguments:
- queries: bfloat16 [1024, 64, 128], P('ctx', 'grp'), parts along dimension 1, may hold values from -4.6 to 4.6
- keys: bfloat16 [1024, 512], P('ctx', 'grp'), parts along dimension 1, may hold values from -4.6 to 4.6
- values: bfloat16 [1024, 512], P('ctx', 'grp'), parts along dimension 1, may hold values from -6 to 6
- grad_out: bfloat16 [1024, 64, 128], P('ctx', 'grp'), parts along dimension 1, may hold values from -6 to 6
- lengths: int32 [16], replicated, may hold values from 1 to 640, 1024 in all
Outputs:
- grad_queries: bfloat16 [1024, 64, 128], P('ctx', 'grp'), parts along dimension 1
- grad_keys: bfloat16 [1024, 512], P('ctx', 'grp'), parts along dimension 1
- grad_values: bfloat16 [1024, 512], P('ctx', 'grp'), parts along dimension 1
The draws below stay inside these ranges and needn't reach their ends.
There are 4 independent parts, one for each index of `grp`. The reference program is written for one: setup_inputs(seed, part) draws one part's arguments, and reference() takes and returns one part's arrays. A program takes and returns all parts, laid end to end along the dimension named above; an argument that names none is the same for every part. Nothing has to cross between parts.
Inputs may be any that keep to these rules, and one draw needn't show every extreme that they name: `lengths`: the 16 documents lie end to end in the given order and fill the pack; the longest has exactly 640 tokens.
All inputs are finite; a program needn't handle non-finite values.
Results may differ from the reference program's by a relative error of at most 0.015.
Values may be sent and summed in bfloat16 or wider, within the bound.
No kernel may reach another device: no remote copies, remote signals or barrier semaphores. Data moves between devices by JAX's collectives and lax.ppermute only.
A program may use at most 64 MiB of HBM per device.

```python
import math
import jax
import jax.numpy as jnp
import numpy as np
from jax import lax

HEADS = 16
HD = 128
NDOCS = 16
LENGTH = 1024
MOST_DOC = 640


def draw_pair(key):
    base = jax.random.fold_in(key, 11)
    key_query, key_key = jax.random.split(base, 2)
    query_mat = jnp.clip(jax.random.normal(key_query, (LENGTH, HEADS, HD), jnp.float32), -4.6, 4.6)
    key_mat = jnp.clip(jax.random.normal(key_key, (LENGTH, HD), jnp.float32), -4.6, 4.6)
    return (query_mat, key_mat)


def draw_queries(key, part):
    return draw_pair(key)[0].astype(jnp.bfloat16)


def draw_keys(key, part):
    return draw_pair(key)[1].astype(jnp.bfloat16)


def block_levels(key, extent, cuts, least, high):
    gain, own = 1.0, jax.random.fold_in(key, 6)
    for dim, shards_of in cuts:
        draws = jnp.exp(jax.random.uniform(jax.random.fold_in(own, dim), (shards_of,), jnp.float32, least / len(cuts), high / len(cuts)))
        gain = gain * jnp.repeat(draws, extent[dim] // shards_of).reshape([-1 if axis == dim else 1 for axis in range(len(extent))])
    return gain


def length_profile(count, total, bound, skew):
    portions = [(1 << 20) // math.isqrt(rank ** skew) + 1 for rank in range(2, count + 1)]
    rest, holding = total - bound - (count - 1), [1] * (count - 1)
    while rest > 0:
        free = [i for i in range(count - 1) if holding[i] < bound]
        whole, budget = sum([portions[i] for i in free]), rest
        for i in free:
            extra = min(bound - holding[i], max(1, budget * portions[i] // whole), rest)
            holding[i] = holding[i] + extra
            rest = rest - extra
    return np.array([bound] + holding)


def uneven_parts(key, count, total, limit, skew):
    if count == 2:
        one = jax.random.randint(key, (), max(1, total - limit), min(limit, total - 1) + 1)
        return jnp.stack([one, total - one])
    sizes = jnp.asarray(length_profile(count, total, limit, skew), jnp.int32)
    couples = (count - 1) // 2
    donor, sink = sizes[1:1 + 2 * couples:2], sizes[2:2 + 2 * couples:2]
    room = jnp.minimum(donor - 1, limit - sink)
    passed = jax.random.randint(jax.random.fold_in(key, 1), (couples,), 0, 1 << 20) % (room + 1)
    sizes = sizes.at[1:1 + 2 * couples:2].set(donor - passed).at[2:2 + 2 * couples:2].set(sink + passed)
    return sizes[jax.random.permutation(jax.random.fold_in(key, 2), count)]


def normal_values(rng, extent, width, limit, cuts=(), kind=jnp.bfloat16):
    drawn = width * jax.random.normal(rng, extent, jnp.float32)
    if cuts:
        drawn = drawn * block_levels(rng, extent, cuts, -0.22, 0.18)
    return jnp.clip(drawn, -limit, limit).astype(kind)


def setup_inputs(seed: int = 0, part: int = 0) -> dict:
    seeds = jax.random.split(jax.random.key(seed), 6)
    own_keys = jax.random.split(jax.random.fold_in(seeds[5], part), 6)
    return {
        "queries": draw_queries(jax.random.fold_in(jax.random.fold_in(seeds[5], part), 71), part),
        "keys": draw_keys(jax.random.fold_in(jax.random.fold_in(seeds[5], part), 71), part),
        "values": normal_values(own_keys[2], (LENGTH, HD), 1.0, 6.0, ((0, 8),)),
        "grad_out": normal_values(own_keys[3], (LENGTH, HEADS, HD), 1.0, 6.0, ((0, 8),)),
        "lengths": uneven_parts(seeds[4], NDOCS, LENGTH, MOST_DOC, 2).astype(jnp.int32),
    }


def reference(queries, keys, values, grad_out, lengths):
    scale = 1.0 / math.sqrt(HD)
    ends = jnp.cumsum(lengths)
    positions = jnp.arange(LENGTH, dtype=jnp.int32)
    documents = lax.optimization_barrier(jnp.sum((positions[:, None] >= ends[None, :]).astype(jnp.int32), axis=1))
    key_full = keys.astype(jnp.float32)
    value_full = values.astype(jnp.float32)
    span = math.gcd(LENGTH, 512)

    def one_block(carry, index):
        start = (index * span).astype(jnp.int32)
        query_block = lax.dynamic_slice_in_dim(queries, start, span, 0).astype(jnp.float32)
        grad_block = lax.dynamic_slice_in_dim(grad_out, start, span, 0).astype(jnp.float32)
        query_pos = lax.dynamic_slice_in_dim(positions, start, span, 0)
        query_doc = lax.dynamic_slice_in_dim(documents, start, span, 0)
        allowed = ((query_doc[:, None] == documents[None, :]) & (positions[None, :] <= query_pos[:, None]))[:, None, :]
        scores = jnp.einsum('thd,ld->thl', query_block, key_full) * scale
        top = lax.optimization_barrier(jnp.max(jnp.where(allowed, scores, -jnp.inf), axis=-1, keepdims=True))
        total = lax.optimization_barrier(jnp.sum(jnp.where(allowed, jnp.exp(scores - top), 0.0), axis=-1, keepdims=True))
        lse = top + jnp.log(total)
        probs = jnp.where(allowed, jnp.exp(scores - lse), 0.0)
        probs_half = lax.optimization_barrier(probs.astype(jnp.bfloat16)).astype(jnp.float32)
        output = jnp.einsum('thl,ld->thd', probs_half, value_full)
        output = lax.optimization_barrier(output.astype(jnp.bfloat16)).astype(jnp.float32)
        delta = lax.optimization_barrier(jnp.sum(grad_block * output, axis=-1, keepdims=True))
        grad_probs = jnp.einsum('thd,ld->thl', grad_block, value_full)
        grad_scores = lax.optimization_barrier((scale * probs * (grad_probs - delta)).astype(jnp.bfloat16)).astype(jnp.float32)
        grad_query = jnp.einsum('thl,ld->thd', grad_scores, key_full).astype(jnp.bfloat16)
        grad_key = carry[0] + jnp.einsum('thl,thd->ld', grad_scores, query_block)
        grad_value = carry[1] + jnp.einsum('thl,thd->ld', probs_half, grad_block)
        return ((grad_key, grad_value), grad_query)
    zeros = jnp.zeros((LENGTH, HD), jnp.float32)
    sums, stacked = lax.scan(one_block, (zeros, zeros), jnp.arange(LENGTH // span, dtype=jnp.int32))
    grad_queries = stacked.reshape(LENGTH, HEADS, HD)
    return (grad_queries, sums[0].astype(jnp.bfloat16), sums[1].astype(jnp.bfloat16))
```

```python
import functools
import math

import jax
import jax.numpy as jnp
from jax import lax
from jax.experimental import pallas as pl
from jax.experimental.pallas import tpu as pltpu
from jax.sharding import PartitionSpec as P

NT = (((1,), (1,)), ((), ()))
TILE = 256


def attend(back, heads, lengths, start, *refs):
    q_ref, g_ref = refs[0], refs[1]
    kv_refs = refs[2 : 3 + back]
    dq_ref, own_ref = refs[3 + back], refs[4 + back]
    sent = refs[5 + back : 5 + 2 * back]
    acc = refs[5 + 2 * back]
    block = kv_refs[0].shape[0] // 2
    width = q_ref.shape[1]
    scale = 1.0 / math.sqrt(width)
    to_exp2 = scale * math.log2(math.e)
    first = start[0]

    def tile(index, carry):
        at = pl.ds(pl.multiple_of(index * TILE, TILE), TILE)
        q, g = q_ref[at, :], g_ref[at, :]
        row = lax.broadcasted_iota(jnp.int32, (1, TILE), 1) + index * TILE
        pos = first + lax.div(row, heads)
        low, end = jnp.zeros_like(pos), jnp.int32(0)
        for n in range(lengths.shape[0]):
            end = end + lengths[n]
            low = jnp.where(end <= pos, jnp.maximum(low, end), low)
        key = lax.broadcasted_iota(jnp.int32, (block, TILE), 0)
        scores, top = [], None
        for b in range(back + 1):
            s = lax.dot_general(kv_refs[b][:block, :], q, NT, preferred_element_type=jnp.float32)
            base = first - b * block
            allowed = (key >= low - base) & (key <= pos - base) if b == 0 else key >= low - base
            s = jnp.where(allowed, s, -1e30)
            high = jnp.max(s, axis=0, keepdims=True)
            top = high if top is None else jnp.maximum(top, high)
            scores.append(s)
        total, weighted, exps, grads = 0.0, 0.0, [], []
        for b in range(back + 1):
            e = jnp.exp2((scores[b] - top) * to_exp2)
            gp = lax.dot_general(kv_refs[b][block:, :], g, NT, preferred_element_type=jnp.float32)
            total = total + jnp.sum(e, axis=0, keepdims=True)
            weighted = weighted + jnp.sum(e * gp, axis=0, keepdims=True)
            exps.append(e)
            grads.append(gp)
        inverse = 1.0 / total
        delta = weighted * inverse
        dq = None
        for b in range(back + 1):
            p = exps[b] * inverse
            ds = (p * (grads[b] - delta)).astype(jnp.bfloat16)
            dk = jnp.dot(ds, q, preferred_element_type=jnp.float32)
            dv = jnp.dot(p.astype(jnp.bfloat16), g, preferred_element_type=jnp.float32)
            acc[b, :block, :] += dk
            acc[b, block:, :] += dv
            part = lax.dot_general(
                ds, kv_refs[b][:block, :], (((0,), (0,)), ((), ())), preferred_element_type=jnp.float32
            )
            dq = part if dq is None else dq + part
        dq_ref[at, :] = (dq * scale).astype(dq_ref.dtype)
        return carry

    acc[...] = jnp.zeros_like(acc)
    lax.fori_loop(0, q_ref.shape[0] // TILE, tile, 0)
    for b in range(back + 1):
        out = own_ref if b == 0 else sent[b - 1]
        out[:block, :] = (acc[b, :block, :] * scale).astype(out.dtype)
        out[block:, :] = acc[b, block:, :].astype(out.dtype)


def combine(*refs):
    own, rest, (dk, dv) = refs[0], refs[1:-2], refs[-2:]
    block = dk.shape[0]
    total = own[...]
    for r in rest:
        total = total + r[...].astype(jnp.float32)
    dk[...] = total[:block].astype(dk.dtype)
    dv[...] = total[block:].astype(dv.dtype)


def on_device(queries, keys, values, grad_out, lengths):
    rows, heads, width = queries.shape
    count = lax.axis_size("ctx")
    longest = rows * count // 2 + rows
    back = min(count - 1, -(-(longest - 1) // rows))
    start = (lax.axis_index("ctx") * rows).astype(jnp.int32).reshape(1)
    vmem, smem = pl.BlockSpec(memory_space=pltpu.VMEM), pl.BlockSpec(memory_space=pltpu.SMEM)

    def turn(x, by):
        return lax.ppermute(x, "ctx", [(i, (i + by) % count) for i in range(count)])

    pair = jnp.concatenate([keys, values], axis=0)
    blocks = [pair] + [turn(pair, b) for b in range(1, back + 1)]
    outs = pl.pallas_call(
        functools.partial(attend, back, heads),
        out_shape=[
            jax.ShapeDtypeStruct((rows * heads, width), jnp.bfloat16),
            jax.ShapeDtypeStruct((2 * rows, width), jnp.float32),
        ]
        + [jax.ShapeDtypeStruct((2 * rows, width), jnp.bfloat16)] * back,
        in_specs=[smem, smem] + [vmem] * (back + 3),
        out_specs=[vmem] * (back + 2),
        scratch_shapes=[pltpu.VMEM((back + 1, 2 * rows, width), jnp.float32)],
        compiler_params=pltpu.CompilerParams(vmem_limit_bytes=48 * 2**20),
    )(lengths, start, queries.reshape(-1, width), grad_out.reshape(-1, width), *blocks)
    returned = [turn(outs[1 + b], -b) for b in range(1, back + 1)]
    dk, dv = pl.pallas_call(
        combine,
        out_shape=[jax.ShapeDtypeStruct((rows, width), jnp.bfloat16)] * 2,
        in_specs=[vmem] * (back + 1),
        out_specs=[vmem] * 2,
    )(outs[1], *returned)
    return outs[0].reshape(queries.shape), dk, dv


def solution(mesh):
    return jax.shard_map(
        on_device,
        mesh=mesh,
        in_specs=(
            P("ctx", "grp", None),
            P("ctx", "grp"),
            P("ctx", "grp"),
            P("ctx", "grp", None),
            P(),
        ),
        out_specs=(P("ctx", "grp", None), P("ctx", "grp"), P("ctx", "grp")),
        check_vma=False,
    )
```

```python
import functools
import math

import jax
import jax.numpy as jnp
from jax import lax
from jax.experimental import pallas as pl
from jax.experimental.pallas import tpu as pltpu
from jax.sharding import PartitionSpec as P

NT = (((1,), (1,)), ((), ()))
TILE = 256
EARLY = 2
F32, BF16 = jnp.float32, jnp.bfloat16
VMEM = pl.BlockSpec(memory_space=pltpu.VMEM)
SMEM = pl.BlockSpec(memory_space=pltpu.SMEM)
FAR = pl.BlockSpec(memory_space=pltpu.HBM)


def shape(*dims, dtype=BF16):
    return jax.ShapeDtypeStruct(dims, dtype)


def call(kernel, outs, scratch=(), mib=8, flops=0, far=()):
    def run(*args):
        in_specs = [FAR if n in far else SMEM if a.ndim == 1 else VMEM for n, a in enumerate(args)]
        args = [pltpu.with_memory_space_constraint(a, pltpu.HBM) if n in far else a for n, a in enumerate(args)]
        return pl.pallas_call(
            kernel,
            out_shape=outs,
            in_specs=in_specs,
            out_specs=[VMEM] * len(outs),
            scratch_shapes=scratch,
            compiler_params=pltpu.CompilerParams(vmem_limit_bytes=mib * 2**20),
            cost_estimate=pl.CostEstimate(flops=flops, bytes_accessed=2**20, transcendentals=0),
        )(*args)

    return run


def doc_begin(pos, lengths):
    low, end = jnp.zeros_like(pos), jnp.int32(0)
    for n in range(lengths.shape[0]):
        end = end + lengths[n]
        low = jnp.where(end <= pos, jnp.maximum(low, end), low)
    return low


def pack_kernel(k_far, v_far, pair_ref, sems):
    block = k_far.shape[0]
    copies = [
        pltpu.make_async_copy(k_far, pair_ref.at[pl.ds(0, block)], sems.at[0]),
        pltpu.make_async_copy(v_far, pair_ref.at[pl.ds(block, block)], sems.at[1]),
    ]
    for c in copies:
        c.start()
    for c in copies:
        c.wait()


def masked_scores(pair_ref, q, low, row, shift):
    block = pair_ref.shape[0] // 2
    key = lax.broadcasted_iota(jnp.int32, (block, q.shape[0]), 0).astype(F32)
    s = lax.dot_general(pair_ref[:block, :], q, NT, preferred_element_type=F32)
    allowed = key >= low + float(shift * block)
    if shift == 0:
        allowed = allowed & (key <= row)
    return jnp.where(allowed, s, -1e30)


def early_kernel(shifts, heads, to_exp2, start, lengths_far, q_far, g_far, *refs):
    pairs = refs[: len(shifts)]
    q_ref, g_ref, e_ref, gp_ref, stat_ref, lengths, q_sems, g_sems, len_sem = refs[len(shifts) :]
    block = pairs[0].shape[0] // 2
    first = start[0]
    tiles = q_ref.shape[0] // TILE
    len_copy = pltpu.make_async_copy(lengths_far, lengths, len_sem)
    len_copy.start()
    copies = []
    for index in range(tiles):
        at = pl.ds(index * TILE, TILE)
        copies.append(
            (
                pltpu.make_async_copy(q_far.at[at], q_ref.at[at], q_sems.at[index]),
                pltpu.make_async_copy(g_far.at[at], g_ref.at[at], g_sems.at[index]),
            )
        )
        for c in copies[-1]:
            c.start()
    len_copy.wait()
    for index in range(tiles):
        at = pl.ds(index * TILE, TILE)
        row = lax.div(lax.broadcasted_iota(jnp.int32, (1, TILE), 1) + index * TILE, heads)
        low = (doc_begin(first + row, lengths) - first).astype(F32)
        row = row.astype(F32)
        for c in copies[index]:
            c.wait()
        q, g = q_ref[at, :], g_ref[at, :]
        scores, top = [], None
        for n, shift in enumerate(shifts):
            s = masked_scores(pairs[n], q, low, row, shift)
            high = jnp.max(s, axis=0, keepdims=True)
            top = high if top is None else jnp.maximum(top, high)
            scores.append(s)
        total, weighted = 0.0, 0.0
        for n in range(len(shifts)):
            e = jnp.exp2((scores[n] - top) * to_exp2)
            gp = lax.dot_general(pairs[n][block:, :], g, NT, preferred_element_type=F32)
            total = total + jnp.sum(e, axis=0, keepdims=True)
            weighted = weighted + jnp.sum(e * gp, axis=0, keepdims=True)
            e_ref[n * block : (n + 1) * block, at] = e
            gp_ref[n * block : (n + 1) * block, at] = gp
        stat_ref[0:1, at] = top
        stat_ref[1:2, at] = total
        stat_ref[2:3, at] = weighted
        stat_ref[3:4, at] = low


def main_kernel(early, late, scale, to_exp2, *refs):
    q_ref, g_ref, e_ref, gp_ref, stat_ref = refs[:5]
    pairs = refs[5 : 5 + len(late)]
    p_own, ds_ref = refs[5 + len(late) : 7 + len(late)]
    sent = refs[7 + len(late) : -2]
    p_ref, acc = refs[-2:]
    back = len(sent)
    block = pairs[0].shape[0] // 2
    tiles = q_ref.shape[0] // TILE

    def keep(shift, at, p, ds):
        if shift == 0:
            p_own[:, at] = p.astype(BF16)
        else:
            p_ref[(shift - 1) * block : shift * block, at] = p.astype(BF16)
        ds_ref[shift * block : (shift + 1) * block, at] = ds.astype(BF16)

    def probabilities(index):
        at = pl.ds(index * TILE, TILE)
        q, g = q_ref[at, :], g_ref[at, :]
        early_top, low = stat_ref[0:1, at], stat_ref[3:4, at]
        top, scores = early_top, []
        for n, shift in enumerate(late):
            s = masked_scores(pairs[n], q, low, None, shift)
            top = jnp.maximum(top, jnp.max(s, axis=0, keepdims=True))
            scores.append(s)
        factor = jnp.exp2((early_top - top) * to_exp2)
        total, weighted = stat_ref[1:2, at] * factor, stat_ref[2:3, at] * factor
        exps, grads = [], []
        for n in range(len(late)):
            e = jnp.exp2((scores[n] - top) * to_exp2)
            gp = lax.dot_general(pairs[n][block:, :], g, NT, preferred_element_type=F32)
            total = total + jnp.sum(e, axis=0, keepdims=True)
            weighted = weighted + jnp.sum(e * gp, axis=0, keepdims=True)
            exps.append(e)
            grads.append(gp)
        inverse = 1.0 / total
        delta = weighted * inverse
        for n, shift in enumerate(early):
            part = slice(n * block, (n + 1) * block)
            p = e_ref[part, at] * (factor * inverse)
            keep(shift, at, p, p * (gp_ref[part, at] - delta))
        for n, shift in enumerate(late):
            p = exps[n] * inverse
            keep(shift, at, p, p * (grads[n] - delta))

    def sums(index):
        at = pl.ds(index * TILE, TILE)
        dk = jnp.dot(ds_ref[block:, at], q_ref[at, :], preferred_element_type=F32)
        dv = jnp.dot(p_ref[:, at], g_ref[at, :], preferred_element_type=F32)
        if index == 0:
            acc[0], acc[1] = dk, dv
        else:
            acc[0] += dk
            acc[1] += dv

    for index in range(tiles):
        probabilities(index)
        if index:
            sums(index - 1)
    sums(tiles - 1)
    for b in range(back):
        at = slice(b * block, (b + 1) * block)
        sent[b][:block, :] = (acc[0, at, :] * scale).astype(BF16)
        sent[b][block:, :] = acc[1, at, :].astype(BF16)


def rest_kernel(back, scale, *refs):
    q_ref, g_ref, p_own, ds_ref = refs[:4]
    pairs, (dq_ref, own_ref, k_ref) = refs[4 : 5 + back], refs[5 + back :]
    block = pairs[0].shape[0] // 2
    for b in range(back + 1):
        k_ref[:, b * block : (b + 1) * block] = pairs[b][:block, :].T
    own_ref[:block, :] = jnp.dot(ds_ref[:block, :], q_ref[...], preferred_element_type=F32) * scale
    own_ref[block:, :] = jnp.dot(p_own[...], g_ref[...], preferred_element_type=F32)
    dq = jnp.dot(k_ref[...], ds_ref[...], preferred_element_type=F32) * scale
    dq_ref[...] = dq.T.astype(BF16)


def combine(own, *refs):
    rest, (dk, dv) = refs[:-2], refs[-2:]
    block = dk.shape[0]
    total = own[...]
    for r in rest:
        total = total + r[...].astype(F32)
    dk[...] = total[:block].astype(BF16)
    dv[...] = total[block:].astype(BF16)


def whole_kernel(back, heads, scale, to_exp2, lengths, start, *refs):
    q_ref, g_ref = refs[0], refs[1]
    pairs = refs[2 : 3 + back]
    dq_ref, own_ref = refs[3 + back], refs[4 + back]
    sent = refs[5 + back : 5 + 2 * back]
    acc = refs[5 + 2 * back]
    block = pairs[0].shape[0] // 2
    first = start[0]

    def tile(index, carry):
        at = pl.ds(pl.multiple_of(index * TILE, TILE), TILE)
        q, g = q_ref[at, :], g_ref[at, :]
        row = lax.div(lax.broadcasted_iota(jnp.int32, (1, TILE), 1) + index * TILE, heads)
        low = doc_begin(first + row, lengths) - first
        key = lax.broadcasted_iota(jnp.int32, (block, TILE), 0)
        scores, top = [], None
        for b in range(back + 1):
            s = lax.dot_general(pairs[b][:block, :], q, NT, preferred_element_type=F32)
            allowed = (key >= low) & (key <= row) if b == 0 else key >= low + b * block
            s = jnp.where(allowed, s, -1e30)
            high = jnp.max(s, axis=0, keepdims=True)
            top = high if top is None else jnp.maximum(top, high)
            scores.append(s)
        total, weighted, exps, grads = 0.0, 0.0, [], []
        for b in range(back + 1):
            e = jnp.exp2((scores[b] - top) * to_exp2)
            gp = lax.dot_general(pairs[b][block:, :], g, NT, preferred_element_type=F32)
            total = total + jnp.sum(e, axis=0, keepdims=True)
            weighted = weighted + jnp.sum(e * gp, axis=0, keepdims=True)
            exps.append(e)
            grads.append(gp)
        inverse = 1.0 / total
        delta = weighted * inverse
        dq = None
        for b in range(back + 1):
            p = exps[b] * inverse
            ds = (p * (grads[b] - delta)).astype(BF16)
            acc[b, :block, :] += jnp.dot(ds, q, preferred_element_type=F32)
            acc[b, block:, :] += jnp.dot(p.astype(BF16), g, preferred_element_type=F32)
            part = lax.dot_general(
                ds, pairs[b][:block, :], (((0,), (0,)), ((), ())), preferred_element_type=F32
            )
            dq = part if dq is None else dq + part
        dq_ref[at, :] = (dq * scale).astype(BF16)
        return carry

    acc[...] = jnp.zeros_like(acc)
    lax.fori_loop(0, q_ref.shape[0] // TILE, tile, 0)
    for b in range(back + 1):
        out = own_ref if b == 0 else sent[b - 1]
        out[:block, :] = (acc[b, :block, :] * scale).astype(out.dtype)
        out[block:, :] = acc[b, block:, :].astype(out.dtype)


def on_device(queries, keys, values, grad_out, lengths):
    rows, heads, width = queries.shape
    count = lax.axis_size("ctx")
    longest = rows * count // 2 + rows
    back = min(count - 1, -(-(longest - 1) // rows))
    start = (lax.axis_index("ctx") * rows).astype(jnp.int32).reshape(1)
    scale = 1.0 / math.sqrt(width)
    to_exp2 = scale * math.log2(math.e)
    q, g = queries.reshape(-1, width), grad_out.reshape(-1, width)
    flat = rows * heads

    def turn(x, by):
        return lax.ppermute(x, "ctx", [(i, (i + by) % count) for i in range(count)])

    pair = call(pack_kernel, [shape(2 * rows, width)], [pltpu.SemaphoreType.DMA((2,))], mib=1, far=(0, 1))(
        keys, values
    )[0]
    others = [turn(pair, b) for b in range(1, back + 1)]
    partial = shape(2 * rows, width)
    if back > 7:
        dq, own, *sent = call(
            functools.partial(whole_kernel, back, heads, scale, to_exp2),
            [shape(flat, width), shape(2 * rows, width, dtype=F32)] + [partial] * back,
            [pltpu.VMEM((back + 1, 2 * rows, width), F32)],
            mib=48,
        )(lengths, start, q, g, pair, *others)
        returned = [turn(sent[b - 1], -b) for b in range(1, back + 1)]
    else:
        early = (0,) + tuple(range(back, back - EARLY, -1))
        late = tuple(range(1, back + 1 - EARLY))
        tall = len(early) * rows
        tiles = flat // TILE
        q, g, e, gp, stat = call(
            functools.partial(early_kernel, early, heads, to_exp2),
            [
                shape(flat, width),
                shape(flat, width),
                shape(tall, flat, dtype=F32),
                shape(tall, flat, dtype=F32),
                shape(8, flat, dtype=F32),
            ],
            [
                pltpu.SMEM(lengths.shape, jnp.int32),
                pltpu.SemaphoreType.DMA((tiles,)),
                pltpu.SemaphoreType.DMA((tiles,)),
                pltpu.SemaphoreType.DMA,
            ],
            flops=2**29,
            far=(1, 2, 3),
        )(start, lengths, q, g, *([pair, *others][shift] for shift in early))
        p_own, ds, *sent = call(
            functools.partial(main_kernel, early, late, scale, to_exp2),
            [shape(rows, flat), shape((back + 1) * rows, flat)] + [partial] * back,
            [pltpu.VMEM((back * rows, flat), BF16), pltpu.VMEM((2, back * rows, width), F32)],
            mib=16,
            flops=2**31,
        )(q, g, e, gp, stat, *(others[shift - 1] for shift in late))
        returned = [turn(sent[b - 1], -b) for b in range(1, back + 1)]
        dq, own = call(
            functools.partial(rest_kernel, back, scale),
            [shape(flat, width), shape(2 * rows, width, dtype=F32)],
            [pltpu.VMEM((width, (back + 1) * rows), BF16)],
            flops=2**29,
        )(q, g, p_own, ds, pair, *others)
    dk, dv = call(combine, [shape(rows, width)] * 2, mib=4)(own, *returned)
    return dq.reshape(queries.shape), dk, dv


def solution(mesh):
    return jax.shard_map(
        on_device,
        mesh=mesh,
        in_specs=(
            P("ctx", "grp", None),
            P("ctx", "grp"),
            P("ctx", "grp"),
            P("ctx", "grp", None),
            P(),
        ),
        out_specs=(P("ctx", "grp", None), P("ctx", "grp"), P("ctx", "grp")),
        check_vma=False,
    )
```

```python
import functools
import math

import jax
import jax.numpy as jnp
from jax import lax
from jax.experimental import pallas as pl
from jax.experimental.pallas import tpu as pltpu
from jax.sharding import PartitionSpec as P

NT = (((1,), (1,)), ((), ()))
TILE = 256
EARLY = 2
F32, BF16 = jnp.float32, jnp.bfloat16
VMEM = pl.BlockSpec(memory_space=pltpu.VMEM)
SMEM = pl.BlockSpec(memory_space=pltpu.SMEM)
FAR = pl.BlockSpec(memory_space=pltpu.HBM)


def shape(*dims, dtype=BF16):
    return jax.ShapeDtypeStruct(dims, dtype)


def call(kernel, outs, scratch=(), mib=8, flops=0, far=()):
    def run(*args):
        in_specs = [FAR if n in far else SMEM if a.ndim == 1 else VMEM for n, a in enumerate(args)]
        args = [pltpu.with_memory_space_constraint(a, pltpu.HBM) if n in far else a for n, a in enumerate(args)]
        return pl.pallas_call(
            kernel,
            out_shape=outs,
            in_specs=in_specs,
            out_specs=[VMEM] * len(outs),
            scratch_shapes=scratch,
            compiler_params=pltpu.CompilerParams(vmem_limit_bytes=mib * 2**20),
            cost_estimate=pl.CostEstimate(flops=flops, bytes_accessed=2**20, transcendentals=0),
        )(*args)

    return run


def doc_begin(pos, lengths):
    low, end = jnp.zeros_like(pos), jnp.int32(0)
    for n in range(lengths.shape[0]):
        end = end + lengths[n]
        low = jnp.where(end <= pos, jnp.maximum(low, end), low)
    return low


def pack_kernel(k_far, v_far, pair_ref, sems):
    block = k_far.shape[0]
    copies = [
        pltpu.make_async_copy(k_far, pair_ref.at[pl.ds(0, block)], sems.at[0]),
        pltpu.make_async_copy(v_far, pair_ref.at[pl.ds(block, block)], sems.at[1]),
    ]
    for c in copies:
        c.start()
    for c in copies:
        c.wait()


def masked_scores(pair_ref, q, low, row, shift):
    block = pair_ref.shape[0] // 2
    key = lax.broadcasted_iota(jnp.int32, (block, q.shape[0]), 0).astype(F32)
    s = lax.dot_general(pair_ref[:block, :], q, NT, preferred_element_type=F32)
    allowed = key >= low + float(shift * block)
    if shift == 0:
        allowed = allowed & (key <= row)
    return jnp.where(allowed, s, -1e30)


def block_terms(pairs, shifts, q, g, low, row, top, to_exp2):
    block = pairs[0].shape[0] // 2
    scores = []
    for n, shift in enumerate(shifts):
        s = masked_scores(pairs[n], q, low, row, shift)
        high = jnp.max(s, axis=0, keepdims=True)
        top = high if top is None else jnp.maximum(top, high)
        scores.append(s)
    total, weighted, exps, grads = 0.0, 0.0, [], []
    for n in range(len(shifts)):
        e = jnp.exp2((scores[n] - top) * to_exp2)
        gp = lax.dot_general(pairs[n][block:, :], g, NT, preferred_element_type=F32)
        total = total + jnp.sum(e, axis=0, keepdims=True)
        weighted = weighted + jnp.sum(e * gp, axis=0, keepdims=True)
        exps.append(e)
        grads.append(gp)
    return exps, grads, top, total, weighted


def own_kernel(heads, to_exp2, start, lengths_far, q_far, g_far, pair_ref, *refs):
    q_ref, g_ref, e_ref, gp_ref, stat_ref, lengths, q_sems, g_sems, len_sem = refs
    first = start[0]
    tiles = q_ref.shape[0] // TILE
    len_copy = pltpu.make_async_copy(lengths_far, lengths, len_sem)
    len_copy.start()
    copies = []
    for index in range(tiles):
        at = pl.ds(index * TILE, TILE)
        copies.append(
            (
                pltpu.make_async_copy(q_far.at[at], q_ref.at[at], q_sems.at[index]),
                pltpu.make_async_copy(g_far.at[at], g_ref.at[at], g_sems.at[index]),
            )
        )
        for c in copies[-1]:
            c.start()
    len_copy.wait()
    for index in range(tiles):
        at = pl.ds(index * TILE, TILE)
        row = lax.div(lax.broadcasted_iota(jnp.int32, (1, TILE), 1) + index * TILE, heads)
        low = (doc_begin(first + row, lengths) - first).astype(F32)
        for c in copies[index]:
            c.wait()
        exps, grads, top, total, weighted = block_terms(
            [pair_ref], (0,), q_ref[at, :], g_ref[at, :], low, row.astype(F32), None, to_exp2
        )
        e_ref[:, at] = exps[0]
        gp_ref[:, at] = grads[0]
        for n, value in enumerate((top, total, weighted, low)):
            stat_ref[n : n + 1, at] = value


def next_kernel(shifts, to_exp2, q_ref, g_ref, stat_ref, *refs):
    pairs, (e_ref, gp_ref, out_ref) = refs[: len(shifts)], refs[len(shifts) :]
    block = pairs[0].shape[0] // 2
    for index in range(q_ref.shape[0] // TILE):
        at = pl.ds(index * TILE, TILE)
        old, low = stat_ref[0:1, at], stat_ref[3:4, at]
        exps, grads, top, total, weighted = block_terms(
            pairs, shifts, q_ref[at, :], g_ref[at, :], low, None, old, to_exp2
        )
        factor = jnp.exp2((old - top) * to_exp2)
        for n in range(len(shifts)):
            e_ref[n * block : (n + 1) * block, at] = exps[n]
            gp_ref[n * block : (n + 1) * block, at] = grads[n]
        total = total + stat_ref[1:2, at] * factor
        weighted = weighted + stat_ref[2:3, at] * factor
        for n, value in enumerate((top, total, weighted, low, old)):
            out_ref[n : n + 1, at] = value


def main_kernel(early, late, scale, to_exp2, *refs):
    q_ref, g_ref, e_own, gp_own, e_ref, gp_ref, stat_ref = refs[:7]
    pairs = refs[7 : 7 + len(late)]
    p_own, ds_ref = refs[7 + len(late) : 9 + len(late)]
    sent = refs[9 + len(late) : -2]
    p_ref, acc = refs[-2:]
    back = len(sent)
    block = pairs[0].shape[0] // 2
    tiles = q_ref.shape[0] // TILE

    def keep(shift, at, p, ds):
        if shift == 0:
            p_own[:, at] = p.astype(BF16)
        else:
            p_ref[(shift - 1) * block : shift * block, at] = p.astype(BF16)
        ds_ref[shift * block : (shift + 1) * block, at] = ds.astype(BF16)

    def probabilities(index):
        at = pl.ds(index * TILE, TILE)
        old, low, own_top = stat_ref[0:1, at], stat_ref[3:4, at], stat_ref[4:5, at]
        exps, grads, top, total, weighted = block_terms(
            pairs, late, q_ref[at, :], g_ref[at, :], low, None, old, to_exp2
        )
        factor = jnp.exp2((old - top) * to_exp2)
        inverse = 1.0 / (total + stat_ref[1:2, at] * factor)
        delta = (weighted + stat_ref[2:3, at] * factor) * inverse
        p = e_own[:, at] * (jnp.exp2((own_top - top) * to_exp2) * inverse)
        keep(0, at, p, p * (gp_own[:, at] - delta))
        factor = factor * inverse
        for n, shift in enumerate(early):
            part = slice(n * block, (n + 1) * block)
            p = e_ref[part, at] * factor
            keep(shift, at, p, p * (gp_ref[part, at] - delta))
        for n, shift in enumerate(late):
            p = exps[n] * inverse
            keep(shift, at, p, p * (grads[n] - delta))

    def sums(index):
        at = pl.ds(index * TILE, TILE)
        dk = jnp.dot(ds_ref[block:, at], q_ref[at, :], preferred_element_type=F32)
        dv = jnp.dot(p_ref[:, at], g_ref[at, :], preferred_element_type=F32)
        if index == 0:
            acc[0], acc[1] = dk, dv
        else:
            acc[0] += dk
            acc[1] += dv

    for index in range(tiles):
        probabilities(index)
        if index:
            sums(index - 1)
    sums(tiles - 1)
    for b in range(back):
        at = slice(b * block, (b + 1) * block)
        out = sent[back - 1 - b]
        out[:block, :] = (acc[0, at, :] * scale).astype(BF16)
        out[block:, :] = acc[1, at, :].astype(BF16)


def rest_kernel(back, scale, *refs):
    q_ref, g_ref, p_own, ds_ref = refs[:4]
    pairs, (dq_ref, own_ref, k_ref) = refs[4 : 5 + back], refs[5 + back :]
    block = pairs[0].shape[0] // 2
    for b in range(back + 1):
        k_ref[:, b * block : (b + 1) * block] = pairs[b][:block, :].T
    own_ref[:block, :] = jnp.dot(ds_ref[:block, :], q_ref[...], preferred_element_type=F32) * scale
    own_ref[block:, :] = jnp.dot(p_own[...], g_ref[...], preferred_element_type=F32)
    dq = jnp.dot(k_ref[...], ds_ref[...], preferred_element_type=F32) * scale
    dq_ref[...] = dq.T.astype(BF16)


def combine(own, *refs):
    rest, (dk, dv) = refs[:-2], refs[-2:]
    block = dk.shape[0]
    total = own[...]
    for r in rest:
        total = total + r[...].astype(F32)
    dk[...] = total[:block].astype(BF16)
    dv[...] = total[block:].astype(BF16)


def whole_kernel(back, heads, scale, to_exp2, lengths, start, *refs):
    q_ref, g_ref = refs[0], refs[1]
    pairs = refs[2 : 3 + back]
    dq_ref, own_ref = refs[3 + back], refs[4 + back]
    sent = refs[5 + back : 5 + 2 * back]
    acc = refs[5 + 2 * back]
    block = pairs[0].shape[0] // 2
    first = start[0]

    def tile(index, carry):
        at = pl.ds(pl.multiple_of(index * TILE, TILE), TILE)
        q, g = q_ref[at, :], g_ref[at, :]
        row = lax.div(lax.broadcasted_iota(jnp.int32, (1, TILE), 1) + index * TILE, heads)
        low = doc_begin(first + row, lengths) - first
        key = lax.broadcasted_iota(jnp.int32, (block, TILE), 0)
        scores, top = [], None
        for b in range(back + 1):
            s = lax.dot_general(pairs[b][:block, :], q, NT, preferred_element_type=F32)
            allowed = (key >= low) & (key <= row) if b == 0 else key >= low + b * block
            s = jnp.where(allowed, s, -1e30)
            high = jnp.max(s, axis=0, keepdims=True)
            top = high if top is None else jnp.maximum(top, high)
            scores.append(s)
        total, weighted, exps, grads = 0.0, 0.0, [], []
        for b in range(back + 1):
            e = jnp.exp2((scores[b] - top) * to_exp2)
            gp = lax.dot_general(pairs[b][block:, :], g, NT, preferred_element_type=F32)
            total = total + jnp.sum(e, axis=0, keepdims=True)
            weighted = weighted + jnp.sum(e * gp, axis=0, keepdims=True)
            exps.append(e)
            grads.append(gp)
        inverse = 1.0 / total
        delta = weighted * inverse
        dq = None
        for b in range(back + 1):
            p = exps[b] * inverse
            ds = (p * (grads[b] - delta)).astype(BF16)
            acc[b, :block, :] += jnp.dot(ds, q, preferred_element_type=F32)
            acc[b, block:, :] += jnp.dot(p.astype(BF16), g, preferred_element_type=F32)
            part = lax.dot_general(
                ds, pairs[b][:block, :], (((0,), (0,)), ((), ())), preferred_element_type=F32
            )
            dq = part if dq is None else dq + part
        dq_ref[at, :] = (dq * scale).astype(BF16)
        return carry

    acc[...] = jnp.zeros_like(acc)
    lax.fori_loop(0, q_ref.shape[0] // TILE, tile, 0)
    for b in range(back + 1):
        out = own_ref if b == 0 else sent[b - 1]
        out[:block, :] = (acc[b, :block, :] * scale).astype(out.dtype)
        out[block:, :] = acc[b, block:, :].astype(out.dtype)


def on_device(queries, keys, values, grad_out, lengths):
    rows, heads, width = queries.shape
    count = lax.axis_size("ctx")
    longest = rows * count // 2 + rows
    back = min(count - 1, -(-(longest - 1) // rows))
    start = (lax.axis_index("ctx") * rows).astype(jnp.int32).reshape(1)
    scale = 1.0 / math.sqrt(width)
    to_exp2 = scale * math.log2(math.e)
    q, g = queries.reshape(-1, width), grad_out.reshape(-1, width)
    flat = rows * heads

    def turn(x, by):
        return lax.ppermute(x, "ctx", [(i, (i + by) % count) for i in range(count)])

    pair = call(pack_kernel, [shape(2 * rows, width)], [pltpu.SemaphoreType.DMA((2,))], mib=1, far=(0, 1))(
        keys, values
    )[0]
    others = [turn(pair, b) for b in range(1, back + 1)]
    partial = shape(2 * rows, width)
    if back > 7:
        dq, own, *sent = call(
            functools.partial(whole_kernel, back, heads, scale, to_exp2),
            [shape(flat, width), shape(2 * rows, width, dtype=F32)] + [partial] * back,
            [pltpu.VMEM((back + 1, 2 * rows, width), F32)],
            mib=48,
        )(lengths, start, q, g, pair, *others)
        returned = [turn(sent[b - 1], -b) for b in range(1, back + 1)]
    else:
        early = tuple(range(back, back - EARLY, -1))
        late = tuple(range(1, back + 1 - EARLY))
        tiles = flat // TILE

        def wide(n):
            return shape(n * rows, flat, dtype=F32)

        q, g, e_own, gp_own, stat = call(
            functools.partial(own_kernel, heads, to_exp2),
            [shape(flat, width), shape(flat, width), wide(1), wide(1), shape(8, flat, dtype=F32)],
            [
                pltpu.SMEM(lengths.shape, jnp.int32),
                pltpu.SemaphoreType.DMA((tiles,)),
                pltpu.SemaphoreType.DMA((tiles,)),
                pltpu.SemaphoreType.DMA,
            ],
            flops=2**28,
            far=(1, 2, 3),
        )(start, lengths, q, g, pair)
        e, gp, stat = call(
            functools.partial(next_kernel, early, to_exp2),
            [wide(EARLY), wide(EARLY), shape(8, flat, dtype=F32)],
            flops=2**28,
        )(q, g, stat, *(others[shift - 1] for shift in early))
        p_own, ds, *sent = call(
            functools.partial(main_kernel, early, late, scale, to_exp2),
            [shape(rows, flat), shape((back + 1) * rows, flat)] + [partial] * back,
            [pltpu.VMEM((back * rows, flat), BF16), pltpu.VMEM((2, back * rows, width), F32)],
            mib=16,
            flops=2**31,
        )(q, g, e_own, gp_own, e, gp, stat, *(others[shift - 1] for shift in late))
        returned = [turn(sent[back - b], -b) for b in range(back, 0, -1)]
        dq, own = call(
            functools.partial(rest_kernel, back, scale),
            [shape(flat, width), shape(2 * rows, width, dtype=F32)],
            [pltpu.VMEM((width, (back + 1) * rows), BF16)],
            flops=2**29,
        )(q, g, p_own, ds, pair, *others)
    dk, dv = call(combine, [shape(rows, width)] * 2, mib=4)(own, *returned)
    return dq.reshape(queries.shape), dk, dv


def solution(mesh):
    return jax.shard_map(
        on_device,
        mesh=mesh,
        in_specs=(
            P("ctx", "grp", None),
            P("ctx", "grp"),
            P("ctx", "grp"),
            P("ctx", "grp", None),
            P(),
        ),
        out_specs=(P("ctx", "grp", None), P("ctx", "grp"), P("ctx", "grp")),
        check_vma=False,
    )
```

```python
import functools
import math

import jax
import jax.numpy as jnp
from jax import lax
from jax.experimental import pallas as pl
from jax.experimental.pallas import tpu as pltpu
from jax.sharding import PartitionSpec as P

NT = (((1,), (1,)), ((), ()))
TILE = 256
GROUPS = ((0, 1), (2, 3))
F32, BF16 = jnp.float32, jnp.bfloat16
VMEM = pl.BlockSpec(memory_space=pltpu.VMEM)
SMEM = pl.BlockSpec(memory_space=pltpu.SMEM)
FAR = pl.BlockSpec(memory_space=pltpu.HBM)


def shape(*dims, dtype=BF16):
    return jax.ShapeDtypeStruct(dims, dtype)


def call(kernel, outs, scratch=(), mib=8, flops=0, far=()):
    def run(*args):
        in_specs = [FAR if n in far else SMEM if a.ndim == 1 else VMEM for n, a in enumerate(args)]
        args = [pltpu.with_memory_space_constraint(a, pltpu.HBM) if n in far else a for n, a in enumerate(args)]
        return pl.pallas_call(
            kernel,
            out_shape=outs,
            in_specs=in_specs,
            out_specs=[VMEM] * len(outs),
            scratch_shapes=scratch,
            compiler_params=pltpu.CompilerParams(vmem_limit_bytes=mib * 2**20),
            cost_estimate=pl.CostEstimate(flops=flops, bytes_accessed=2**20, transcendentals=0),
        )(*args)

    return run


def doc_begin(pos, lengths):
    low, end = jnp.zeros_like(pos), jnp.int32(0)
    for n in range(lengths.shape[0]):
        end = end + lengths[n]
        low = jnp.where(end <= pos, jnp.maximum(low, end), low)
    return low


def pack_kernel(k_far, v_far, pair_ref, sems):
    block = k_far.shape[0]
    copies = [
        pltpu.make_async_copy(k_far, pair_ref.at[pl.ds(0, block)], sems.at[0]),
        pltpu.make_async_copy(v_far, pair_ref.at[pl.ds(block, block)], sems.at[1]),
    ]
    for c in copies:
        c.start()
    for c in copies:
        c.wait()


def block_terms(pairs, bounds, q, g, row, top, to_exp2):
    block = pairs[0].shape[0] // 2
    key = lax.broadcasted_iota(jnp.int32, (block, q.shape[0]), 0).astype(F32)
    scores = []
    for pair, bound in zip(pairs, bounds):
        s = lax.dot_general(pair[:block, :], q, NT, preferred_element_type=F32)
        allowed = key >= bound
        if row is not None:
            allowed = allowed & (key <= row)
        s = jnp.where(allowed, s, -1e30)
        high = jnp.max(s, axis=0, keepdims=True)
        top = high if top is None else jnp.maximum(top, high)
        scores.append(s)
    total, weighted, exps, grads = 0.0, 0.0, [], []
    for pair, s in zip(pairs, scores):
        e = jnp.exp2((s - top) * to_exp2)
        gp = lax.dot_general(pair[block:, :], g, NT, preferred_element_type=F32)
        total = total + jnp.sum(e, axis=0, keepdims=True)
        weighted = weighted + jnp.sum(e * gp, axis=0, keepdims=True)
        exps.append(e)
        grads.append(gp)
    return exps, grads, top, total, weighted


def own_kernel(heads, shifts, to_exp2, start, lengths_far, q_far, g_far, pair_ref, *refs):
    q_ref, g_ref, e_ref, gp_ref, stat_ref, bound_ref, lengths, q_sems, g_sems, len_sem = refs
    first = start[0]
    block = pair_ref.shape[0] // 2
    offsets = []
    for shift in shifts:
        offset = jnp.int32(0)
        for c, s in enumerate(shift):
            offset = jnp.where(first == c * block, s * block, offset)
        offsets.append(offset)
    tiles = q_ref.shape[0] // TILE
    len_copy = pltpu.make_async_copy(lengths_far, lengths, len_sem)
    len_copy.start()
    copies = []
    for index in range(tiles):
        at = pl.ds(index * TILE, TILE)
        copies.append(
            (
                pltpu.make_async_copy(q_far.at[at], q_ref.at[at], q_sems.at[index]),
                pltpu.make_async_copy(g_far.at[at], g_ref.at[at], g_sems.at[index]),
            )
        )
        for c in copies[-1]:
            c.start()
    len_copy.wait()
    for index in range(tiles):
        at = pl.ds(index * TILE, TILE)
        row = lax.div(lax.broadcasted_iota(jnp.int32, (1, TILE), 1) + index * TILE, heads)
        low = doc_begin(first + row, lengths) - first
        for k, offset in enumerate(offsets):
            bound_ref[k : k + 1, at] = (low + offset).astype(F32)
        for c in copies[index]:
            c.wait()
        exps, grads, top, total, weighted = block_terms(
            [pair_ref], [low.astype(F32)], q_ref[at, :], g_ref[at, :], row.astype(F32), None, to_exp2
        )
        e_ref[:, at] = exps[0]
        gp_ref[:, at] = grads[0]
        for n, value in enumerate((total, weighted, top)):
            stat_ref[n : n + 1, at] = value


def next_kernel(group, depth, to_exp2, q_ref, g_ref, bound_ref, stat_ref, *refs):
    pairs, (e_ref, gp_ref, out_ref) = refs[: len(group)], refs[len(group) :]
    block = pairs[0].shape[0] // 2
    for index in range(q_ref.shape[0] // TILE):
        at = pl.ds(index * TILE, TILE)
        old = stat_ref[1 + depth : 2 + depth, at]
        exps, grads, top, total, weighted = block_terms(
            pairs, [bound_ref[k : k + 1, at] for k in group], q_ref[at, :], g_ref[at, :], None, old, to_exp2
        )
        factor = jnp.exp2((old - top) * to_exp2)
        for n in range(len(group)):
            e_ref[n * block : (n + 1) * block, at] = exps[n]
            gp_ref[n * block : (n + 1) * block, at] = grads[n]
        out_ref[0:1, at] = total + stat_ref[0:1, at] * factor
        out_ref[1:2, at] = weighted + stat_ref[1:2, at] * factor
        out_ref[2 : 2 + depth, at] = stat_ref[2 : 2 + depth, at]
        out_ref[2 + depth : 3 + depth, at] = top


def main_kernel(groups, late, scale, to_exp2, *refs):
    q_ref, g_ref, bound_ref, stat_ref = refs[:4]
    depth = len(groups)
    made = [refs[4 + 2 * n : 6 + 2 * n] for n in range(depth)]
    refs = refs[4 + 2 * depth :]
    pairs = refs[: len(late)]
    p_own, ds_ref = refs[len(late) : 2 + len(late)]
    sent = refs[2 + len(late) : -2]
    p_ref, acc = refs[-2:]
    back = len(sent)
    block = pairs[0].shape[0] // 2
    tiles = q_ref.shape[0] // TILE

    def keep(k, at, p, ds):
        if k < 0:
            p_own[:, at] = p.astype(BF16)
        else:
            p_ref[k * block : (k + 1) * block, at] = p.astype(BF16)
        ds_ref[(k + 1) * block : (k + 2) * block, at] = ds.astype(BF16)

    def probabilities(index):
        at = pl.ds(index * TILE, TILE)
        old = stat_ref[1 + depth : 2 + depth, at]
        exps, grads, top, total, weighted = block_terms(
            pairs, [bound_ref[k : k + 1, at] for k in late], q_ref[at, :], g_ref[at, :], None, old, to_exp2
        )
        factor = jnp.exp2((old - top) * to_exp2)
        inverse = 1.0 / (total + stat_ref[0:1, at] * factor)
        delta = (weighted + stat_ref[1:2, at] * factor) * inverse
        for d, group in enumerate(groups):
            e_ref, gp_ref = made[d]
            factor = jnp.exp2((stat_ref[2 + d : 3 + d, at] - top) * to_exp2) * inverse
            for n, k in enumerate(group):
                part = slice(n * block, (n + 1) * block)
                p = e_ref[part, at] * factor
                keep(k, at, p, p * (gp_ref[part, at] - delta))
        for n, k in enumerate(late):
            p = exps[n] * inverse
            keep(k, at, p, p * (grads[n] - delta))

    def sums(index):
        at = pl.ds(index * TILE, TILE)
        dk = jnp.dot(ds_ref[block:, at], q_ref[at, :], preferred_element_type=F32)
        dv = jnp.dot(p_ref[:, at], g_ref[at, :], preferred_element_type=F32)
        if index == 0:
            acc[0], acc[1] = dk, dv
        else:
            acc[0] += dk
            acc[1] += dv

    for index in range(tiles):
        probabilities(index)
        if index:
            sums(index - 1)
    sums(tiles - 1)
    for b in range(back):
        at = slice(b * block, (b + 1) * block)
        out = sent[b]
        out[:block, :] = (acc[0, at, :] * scale).astype(BF16)
        out[block:, :] = acc[1, at, :].astype(BF16)


def rest_kernel(back, scale, *refs):
    q_ref, g_ref, p_own, ds_ref = refs[:4]
    pairs, (dq_ref, own_ref, k_ref) = refs[4 : 5 + back], refs[5 + back :]
    block = pairs[0].shape[0] // 2
    for b in range(back + 1):
        k_ref[:, b * block : (b + 1) * block] = pairs[b][:block, :].T
    own_ref[:block, :] = jnp.dot(ds_ref[:block, :], q_ref[...], preferred_element_type=F32) * scale
    own_ref[block:, :] = jnp.dot(p_own[...], g_ref[...], preferred_element_type=F32)
    dq = jnp.dot(k_ref[...], ds_ref[...], preferred_element_type=F32) * scale
    dq_ref[...] = dq.T.astype(BF16)


def combine(own, *refs):
    rest, (dk, dv) = refs[:-2], refs[-2:]
    block = dk.shape[0]
    total = own[...]
    for r in rest:
        total = total + r[...].astype(F32)
    dk[...] = total[:block].astype(BF16)
    dv[...] = total[block:].astype(BF16)


def whole_kernel(back, heads, scale, to_exp2, lengths, start, *refs):
    q_ref, g_ref = refs[0], refs[1]
    pairs = refs[2 : 3 + back]
    dq_ref, own_ref = refs[3 + back], refs[4 + back]
    sent = refs[5 + back : 5 + 2 * back]
    acc = refs[5 + 2 * back]
    block = pairs[0].shape[0] // 2
    first = start[0]

    def tile(index, carry):
        at = pl.ds(pl.multiple_of(index * TILE, TILE), TILE)
        q, g = q_ref[at, :], g_ref[at, :]
        row = lax.div(lax.broadcasted_iota(jnp.int32, (1, TILE), 1) + index * TILE, heads)
        low = doc_begin(first + row, lengths) - first
        key = lax.broadcasted_iota(jnp.int32, (block, TILE), 0)
        scores, top = [], None
        for b in range(back + 1):
            s = lax.dot_general(pairs[b][:block, :], q, NT, preferred_element_type=F32)
            allowed = (key >= low) & (key <= row) if b == 0 else key >= low + b * block
            s = jnp.where(allowed, s, -1e30)
            high = jnp.max(s, axis=0, keepdims=True)
            top = high if top is None else jnp.maximum(top, high)
            scores.append(s)
        total, weighted, exps, grads = 0.0, 0.0, [], []
        for b in range(back + 1):
            e = jnp.exp2((scores[b] - top) * to_exp2)
            gp = lax.dot_general(pairs[b][block:, :], g, NT, preferred_element_type=F32)
            total = total + jnp.sum(e, axis=0, keepdims=True)
            weighted = weighted + jnp.sum(e * gp, axis=0, keepdims=True)
            exps.append(e)
            grads.append(gp)
        inverse = 1.0 / total
        delta = weighted * inverse
        dq = None
        for b in range(back + 1):
            p = exps[b] * inverse
            ds = (p * (grads[b] - delta)).astype(BF16)
            acc[b, :block, :] += jnp.dot(ds, q, preferred_element_type=F32)
            acc[b, block:, :] += jnp.dot(p.astype(BF16), g, preferred_element_type=F32)
            part = lax.dot_general(
                ds, pairs[b][:block, :], (((0,), (0,)), ((), ())), preferred_element_type=F32
            )
            dq = part if dq is None else dq + part
        dq_ref[at, :] = (dq * scale).astype(BF16)
        return carry

    acc[...] = jnp.zeros_like(acc)
    lax.fori_loop(0, q_ref.shape[0] // TILE, tile, 0)
    for b in range(back + 1):
        out = own_ref if b == 0 else sent[b - 1]
        out[:block, :] = (acc[b, :block, :] * scale).astype(out.dtype)
        out[block:, :] = acc[b, block:, :].astype(out.dtype)


def on_device(queries, keys, values, grad_out, lengths):
    rows, heads, width = queries.shape
    count = lax.axis_size("ctx")
    longest = rows * count // 2 + rows
    back = min(count - 1, -(-(longest - 1) // rows))
    start = (lax.axis_index("ctx") * rows).astype(jnp.int32).reshape(1)
    scale = 1.0 / math.sqrt(width)
    to_exp2 = scale * math.log2(math.e)
    q, g = queries.reshape(-1, width), grad_out.reshape(-1, width)
    flat = rows * heads

    perms = [[(c + b) % count for c in range(count)] for b in range(back, 0, -1)]
    forth = [list(enumerate(p)) for p in perms]
    here = [[(d, c) for c, d in pairs] for pairs in forth]
    shifts = [[c - dict(pairs)[c] for c in range(count)] for pairs in here]
    shifts = [[s if 0 < s <= back else 2 * count for s in row] for row in shifts]

    def fetch(x, k):
        return lax.ppermute(x, "ctx", forth[k])

    def give_back(x, k):
        return lax.ppermute(x, "ctx", here[k])

    pair = call(pack_kernel, [shape(2 * rows, width)], [pltpu.SemaphoreType.DMA((2,))], mib=1, far=(0, 1))(
        keys, values
    )[0]
    others = [fetch(pair, k) for k in range(back)]
    partial = shape(2 * rows, width)
    if back > 7:
        others = others[::-1]
        dq, own, *sent = call(
            functools.partial(whole_kernel, back, heads, scale, to_exp2),
            [shape(flat, width), shape(2 * rows, width, dtype=F32)] + [partial] * back,
            [pltpu.VMEM((back + 1, 2 * rows, width), F32)],
            mib=48,
        )(lengths, start, q, g, pair, *others)
        returned = [give_back(sent[back - 1 - k], k) for k in range(back)]
    else:
        groups = [(-1,), *GROUPS] if back == 5 else [(-1,)]
        late = [k for k in range(back) if k not in sum(groups, ())]
        tiles = flat // TILE

        def wide(n):
            return shape(n * rows, flat, dtype=F32)

        q, g, e, gp, stat, bound = call(
            functools.partial(own_kernel, heads, shifts, to_exp2),
            [shape(flat, width)] * 2 + [wide(1)] * 2 + [shape(8, flat, dtype=F32)] * 2,
            [
                pltpu.SMEM(lengths.shape, jnp.int32),
                pltpu.SemaphoreType.DMA((tiles,)),
                pltpu.SemaphoreType.DMA((tiles,)),
                pltpu.SemaphoreType.DMA,
            ],
            flops=2**28,
            far=(1, 2, 3),
        )(start, lengths, q, g, pair)
        made = [e, gp]
        for depth, group in enumerate(groups[1:], 1):
            e, gp, stat = call(
                functools.partial(next_kernel, group, depth, to_exp2),
                [wide(len(group))] * 2 + [shape(8, flat, dtype=F32)],
                flops=2**28,
            )(q, g, bound, stat, *(others[k] for k in group))
            made += [e, gp]
        p_own, ds, *sent = call(
            functools.partial(main_kernel, groups, late, scale, to_exp2),
            [shape(rows, flat), shape((back + 1) * rows, flat)] + [partial] * back,
            [pltpu.VMEM((back * rows, flat), BF16), pltpu.VMEM((2, back * rows, width), F32)],
            mib=16,
            flops=2**31,
        )(q, g, bound, stat, *made, *(others[k] for k in late))
        returned = [give_back(sent[k], k) for k in range(back)]
        dq, own = call(
            functools.partial(rest_kernel, back, scale),
            [shape(flat, width), shape(2 * rows, width, dtype=F32)],
            [pltpu.VMEM((width, (back + 1) * rows), BF16)],
            flops=2**29,
        )(q, g, p_own, ds, pair, *others)
    dk, dv = call(combine, [shape(rows, width)] * 2, mib=4)(own, *returned)
    return dq.reshape(queries.shape), dk, dv


def solution(mesh):
    return jax.shard_map(
        on_device,
        mesh=mesh,
        in_specs=(
            P("ctx", "grp", None),
            P("ctx", "grp"),
            P("ctx", "grp"),
            P("ctx", "grp", None),
            P(),
        ),
        out_specs=(P("ctx", "grp", None), P("ctx", "grp"), P("ctx", "grp")),
        check_vma=False,
    )
```
